32 devices in a mesh: dp: 4 (over z), row: 4 (over y, x), col: 2 (over core).
Axes of the slice: x: 2, y: 2, z: 4, core: 2. Of those that a mesh axis runs over, the one named last changes fastest.
Arguments:
- tokens: bfloat16 [16384, 512], P(('dp', 'row'), 'col'), may hold values from -7.2 to 7.2
- cotangent: bfloat16 [16384, 512], P(('dp', 'row'), 'col'), may hold values from -6 to 6
- qkv_weight: float32 [3, 512, 512], P(None, 'row', 'col'), may hold values from -0.25 to 0.25
- proj_weight: float32 [512, 512], P('col', 'row'), may hold values from -3 to 3
- up_weight: float32 [512, 2048], P('row', 'col'), may hold values from -0.25 to 0.25
- down_weight: float32 [2048, 512], P('col', 'row'), may hold values from -0.125 to 0.125
- vectors: float32 [12, 512], P(None, 'col'), may hold values from -0.9 to 3.25, as said below
- qkv_mean: float32 [3, 512, 512], P(None, 'row', 'col'), may hold values from -80 to 80
- qkv_square: float32 [3, 512, 512], P(None, 'row', 'col'), may hold values from 8.192 to 131.072
- proj_mean: float32 [512, 512], P('col', 'row'), may hold values from -6 to 6
- proj_square: float32 [512, 512], P('col', 'row'), may hold values from 0.08192 to 1.31072
- up_mean: float32 [512, 2048], P('row', 'col'), may hold values from -32 to 32
- up_square: float32 [512, 2048], P('row', 'col'), may hold values from 0.98304 to 16.384
- down_mean: float32 [2048, 512], P('col', 'row'), may hold values from -48 to 48
- down_square: float32 [2048, 512], P('col', 'row'), may hold values from 2.94912 to 47.5136
- vector_mean: float32 [12, 512], P(None, 'col'), may hold values from -80 to 80
- vector_square: float32 [12, 512], P(None, 'col'), may hold values from 8.192 to 131.072
Outputs:
- block_out: bfloat16 [16384, 512], P(('dp', 'row'), 'col')
- input_grad: float32 [16384, 512], P(('dp', 'row'), 'col')
- qkv_new: float32 [3, 512, 512], P(None, 'row', 'col')
- qkv_mean_new: float32 [3, 512, 512], P(None, 'row', 'col')
- qkv_square_new: float32 [3, 512, 512], P(None, 'row', 'col')
- proj_new: float32 [512, 512], P('col', 'row')
- proj_mean_new: float32 [512, 512], P('col', 'row')
- proj_square_new: float32 [512, 512], P('col', 'row')
- up_new: float32 [512, 2048], P('row', 'col')
- up_mean_new: float32 [512, 2048], P('row', 'col')
- up_square_new: float32 [512, 2048], P('row', 'col')
- down_new: float32 [2048, 512], P('col', 'row')
- down_mean_new: float32 [2048, 512], P('col', 'row')
- down_square_new: float32 [2048, 512], P('col', 'row')
- vector_new: float32 [12, 512], P(None, 'col')
- vector_mean_new: float32 [12, 512], P(None, 'col')
- vector_square_new: float32 [12, 512], P(None, 'col')
- vector_grad: float32 [12, 512], P(None, 'col')
The draws below stay inside these ranges and needn't reach their ends.
Inputs may be any that keep to these rules, and one draw needn't show every extreme that they name: `vectors`: rows 4 and 6 are positive.
All inputs are finite; a program needn't handle non-finite values.
Results may differ from the reference program's by a relative error of at most 0.013.
The reference program's roundings to bfloat16 on the way count: a program that leaves them out, or rounds other values in their place, can miss the bound.
Values may be sent and summed in bfloat16 or wider, within the bound.
A program may use at most 128 MiB of HBM per device.

```python
import math
import jax
import jax.numpy as jnp
from jax import lax

D = 512
HEADS = 8
HEAD_DIM = 64
FF = 2048
SEQ = 512
STEP = 10
TOKENS = 16384
N_COL = 2


def draw_tokens(key, part):
    key = jax.random.fold_in(key, 11)
    columns = jnp.arange(D, dtype=jnp.float32) / (D - 1)
    base = jnp.clip(jax.random.normal(key, (TOKENS, D), jnp.float32), -4.0, 4.0)
    rising = 0.6 * jnp.exp(jnp.log(3.0) * columns)
    return (base * rising).astype(jnp.bfloat16)


def draw_vectors(key, part):
    key = jax.random.fold_in(key, 23)
    key_noise, key_jitter = jax.random.split(key)
    columns = jnp.arange(D, dtype=jnp.float32) / (D - 1)
    noise = 0.3 * jnp.clip(jax.random.normal(key_noise, (12, D), jnp.float32), -3.0, 3.0)
    rising = 0.6 * jnp.exp(jnp.log(3.0) * columns)
    jitter = jax.random.uniform(key_jitter, (12, D), jnp.float32, 0.8, 1.2)
    row_ids = jnp.arange(12)
    is_gain = (row_ids == 4) | (row_ids == 6)
    return jnp.where(is_gain[:, None], rising[None, :] * jitter, noise).astype(jnp.float32)


def shard_levels(own_key, extent, pieces, smallest, largest):
    factor_of = 1.0
    for position, blocks in pieces:
        draws = jax.random.uniform(jax.random.fold_in(jax.random.fold_in(own_key, 6), position), (blocks,), jnp.float32, smallest / len(pieces), largest / len(pieces))
        factor_of = factor_of * jnp.repeat(jnp.exp(draws), extent[position] // blocks).reshape((-1,) + (1,) * (len(extent) - 1 - position))
    return factor_of


def normal_values(key, shape, spread, bound, shards=(), held_as=jnp.bfloat16):
    gain = shard_levels(key, shape, shards, -0.22, 0.18) if shards else 1.0
    entries = jax.random.normal(key, shape, jnp.float32) * spread * gain
    return jnp.minimum(jnp.maximum(entries, -bound), bound).astype(held_as)


def setup_inputs(seed: int = 0) -> dict:
    streams_of = jax.random.split(jax.random.key(seed), 18)
    tokens = draw_tokens(jax.random.fold_in(streams_of[17], 71), 0)
    cotangent = normal_values(streams_of[1], (TOKENS, D), 1.0, 6.0, ((0, 16), (1, 2)))
    qkv_weight = normal_values(streams_of[2], (3, D, D), D ** -0.5, 0.25, ((1, 4), (2, 2)), jnp.float32)
    proj_weight = normal_values(streams_of[3], (D, D), (D * 4 // SEQ) ** -0.5, 3.0, ((0, 2), (1, 4)), jnp.float32)
    up_weight = normal_values(streams_of[4], (D, FF), D ** -0.5, 0.25, ((0, 4), (1, 2)), jnp.float32)
    down_weight = normal_values(streams_of[5], (FF, D), FF ** -0.5, 0.125, ((0, 2), (1, 4)), jnp.float32)
    vectors = draw_vectors(jax.random.fold_in(streams_of[17], 71), 0)
    qkv_mean = normal_values(streams_of[7], (3, D, D), (0.11 * TOKENS ** 0.5), 80.0, ((1, 4), (2, 2)), jnp.float32)
    qkv_square = jnp.clip(jnp.exp(math.log(131.072) - 2.7725887 * jax.random.uniform(streams_of[8], (3, D, D), jnp.float32) ** shard_levels(streams_of[8], (3, D, D), ((1, 4), (2, 2)), -0.2, 0.2)), 8.192, 131.072)
    proj_mean = normal_values(streams_of[9], (D, D), (0.011 * TOKENS ** 0.5), 6.0, ((0, 2), (1, 4)), jnp.float32)
    proj_square = jnp.clip(jnp.exp(math.log(1.31072) - 2.7725887 * jax.random.uniform(streams_of[10], (D, D), jnp.float32) ** shard_levels(streams_of[10], (D, D), ((0, 2), (1, 4)), -0.2, 0.2)), 0.08192, 1.31072)
    up_mean = normal_values(streams_of[11], (D, FF), (0.04 * TOKENS ** 0.5), 32.0, ((0, 4), (1, 2)), jnp.float32)
    up_square = jnp.clip(jnp.exp(math.log(16.384) - 2.8134108 * jax.random.uniform(streams_of[12], (D, FF), jnp.float32) ** shard_levels(streams_of[12], (D, FF), ((0, 4), (1, 2)), -0.2, 0.2)), 0.98304, 16.384)
    down_mean = normal_values(streams_of[13], (FF, D), (0.066 * TOKENS ** 0.5), 48.0, ((0, 2), (1, 4)), jnp.float32)
    down_square = jnp.clip(jnp.exp(math.log(47.5136) - 2.779509 * jax.random.uniform(streams_of[14], (FF, D), jnp.float32) ** shard_levels(streams_of[14], (FF, D), ((0, 2), (1, 4)), -0.2, 0.2)), 2.94912, 47.5136)
    vector_mean = normal_values(streams_of[15], (12, D), (0.11 * TOKENS ** 0.5), 80.0, ((1, 2),), jnp.float32)
    vector_square = jnp.clip(jnp.exp(math.log(131.072) - 2.7725887 * jax.random.uniform(streams_of[16], (12, D), jnp.float32) ** shard_levels(streams_of[16], (12, D), ((1, 2),), -0.2, 0.2)), 8.192, 131.072)
    return dict(tokens=tokens, cotangent=cotangent, qkv_weight=qkv_weight, proj_weight=proj_weight, up_weight=up_weight, down_weight=down_weight, vectors=vectors, qkv_mean=qkv_mean, qkv_square=qkv_square, proj_mean=proj_mean, proj_square=proj_square, up_mean=up_mean, up_square=up_square, down_mean=down_mean, down_square=down_square, vector_mean=vector_mean, vector_square=vector_square)


@jax.custom_vjp
def low(v):
    return lax.optimization_barrier(v.astype(jnp.bfloat16)).astype(jnp.float32)

@jax.custom_vjp
def low_back(v):
    return v

def low_keep(v):
    return (low(v), None)

def low_pass(kept, grad):
    return (grad,)

def back_keep(v):
    return (v, None)

def back_low(kept, grad):
    return (low(grad),)
low.defvjp(low_keep, low_pass)
low_back.defvjp(back_keep, back_low)
HIGH = lax.Precision.HIGHEST
NORM_EPS = 1e-05
BETA_ONE = 0.9
BETA_TWO = 0.999
ADAM_EPS = 1e-08
DECAY_RATE = 0.01
RATE_QKV = 0.03
RATE_PROJ = 0.3
RATE_UP = 0.03
RATE_DOWN = 0.02
RATE_VECTOR = 0.3

def matmul(left, right):
    return jnp.dot(left, right, precision=HIGH)

def layer_norm(summed, gain_row, shift_row):
    mean_row = lax.optimization_barrier(jnp.mean(summed, -1, keepdims=True))
    centered = summed - mean_row
    variance = lax.optimization_barrier(jnp.mean(centered * centered, -1, keepdims=True))
    return centered * lax.rsqrt(variance + NORM_EPS) * gain_row + shift_row

def unpack(vectors):
    up_bias = vectors[8:12].reshape(4, N_COL, D // N_COL).transpose(1, 0, 2).reshape(FF)
    return (vectors[0], vectors[1], vectors[2], vectors[3], vectors[4], vectors[5], vectors[6], vectors[7], up_bias)

def attend(inputs):
    queries, keys, values = inputs
    scores = low_back(HEAD_DIM ** (-0.5) * jnp.einsum('qhe,khe->hqk', queries, keys, precision=HIGH))
    probability = low(jax.nn.softmax(scores, -1))
    return jnp.einsum('hqk,khe->qhe', probability, values, precision=HIGH)

def forward(params, inputs_block):
    qkv_weight, proj_weight, up_weight, down_weight, vectors = params
    query_bias, value_bias, proj_bias, down_bias, gain_first, shift_first, gain_second, shift_second, up_bias = unpack(vectors)
    w_query = low(qkv_weight[0])
    w_key = low(qkv_weight[1])
    w_value = low(qkv_weight[2])
    w_proj = low(proj_weight)
    w_up = low(up_weight)
    w_down = low(down_weight)
    flat_rows = inputs_block.reshape(-1, D)
    queries = low(low_back(matmul(flat_rows, w_query) + query_bias))
    keys = low(low_back(matmul(flat_rows, w_key)))
    values = low(low_back(matmul(flat_rows, w_value) + value_bias))
    head_shape = (-1, SEQ, HEADS, HEAD_DIM)
    context = lax.map(jax.checkpoint(attend), (queries.reshape(head_shape), keys.reshape(head_shape), values.reshape(head_shape)))
    context = low(low_back(context.reshape(-1, D)))
    first_sum = flat_rows + low_back(matmul(context, w_proj)) + proj_bias
    hidden_first = layer_norm(first_sum, gain_first, shift_first)
    pre_act = low_back(matmul(low(hidden_first), w_up) + up_bias)
    activated = low(jax.nn.gelu(pre_act, approximate=False))
    second_sum = hidden_first + low_back(matmul(activated, w_down)) + down_bias
    return layer_norm(second_sum, gain_second, shift_second).reshape(inputs_block.shape)

def adam_step(weight, mean_old, square_old, gradient, step_rate, decay_rate):
    mean_new = BETA_ONE * mean_old + (1.0 - BETA_ONE) * gradient
    square_new = BETA_TWO * square_old + (1.0 - BETA_TWO) * gradient * gradient
    mean_hat = mean_new / (1.0 - BETA_ONE ** STEP)
    square_hat = square_new / (1.0 - BETA_TWO ** STEP)
    weight_new = weight - step_rate * (mean_hat / (jnp.sqrt(square_hat) + ADAM_EPS) + decay_rate * weight)
    return (weight_new, mean_new, square_new)

def reference(tokens, cotangent, qkv_weight, proj_weight, up_weight, down_weight, vectors, qkv_mean, qkv_square, proj_mean, proj_square, up_mean, up_square, down_mean, down_square, vector_mean, vector_square):
    seq_total = TOKENS // SEQ
    group_size = math.gcd(seq_total, max(1, 4096 // SEQ))
    group_count = seq_total // group_size
    inputs_all = tokens.astype(jnp.float32).reshape(group_count, group_size, SEQ, D)
    cotan_all = cotangent.astype(jnp.float32).reshape(group_count, group_size, SEQ, D)
    params = (qkv_weight, proj_weight, up_weight, down_weight, vectors)

    def one_group(running, member):
        inputs_block, cotan_block = member
        result, pullback = jax.vjp(forward, params, inputs_block)
        grad_params, grad_inputs = pullback(cotan_block)
        running = jax.tree.map(jnp.add, running, grad_params)
        return (running, (result.astype(jnp.bfloat16), grad_inputs))
    zero_grads = jax.tree.map(jnp.zeros_like, params)
    gradients, (outputs, input_grads) = lax.scan(one_group, zero_grads, (inputs_all, cotan_all))
    qkv_out = adam_step(qkv_weight, qkv_mean, qkv_square, gradients[0], RATE_QKV, DECAY_RATE)
    proj_out = adam_step(proj_weight, proj_mean, proj_square, gradients[1], RATE_PROJ, DECAY_RATE)
    up_out = adam_step(up_weight, up_mean, up_square, gradients[2], RATE_UP, DECAY_RATE)
    down_out = adam_step(down_weight, down_mean, down_square, gradients[3], RATE_DOWN, DECAY_RATE)
    vector_out = adam_step(vectors, vector_mean, vector_square, gradients[4], RATE_VECTOR, 0.0)
    return (outputs.reshape(TOKENS, D), input_grads.reshape(TOKENS, D), qkv_out[0], qkv_out[1], qkv_out[2], proj_out[0], proj_out[1], proj_out[2], up_out[0], up_out[1], up_out[2], down_out[0], down_out[1], down_out[2], vector_out[0], vector_out[1], vector_out[2], gradients[4])
```

```python
import functools

import jax
import jax.numpy as jnp
from jax import lax
from jax.experimental import pallas as pl
from jax.experimental.pallas import tpu as pltpu
from jax.sharding import PartitionSpec as P

MESH = pl.DeviceIdType.MESH
BF = jnp.bfloat16
F32 = jnp.float32

D = 512
HEADS = 8
HEAD_DIM = 64
FF = 2048
SEQ = 512
STEP = 10
ROWS = 4
HALF = D // 2
BLK = D // ROWS
HID = 512

NORM_EPS = 1e-05
BETA_ONE = 0.9
BETA_TWO = 0.999
ADAM_EPS = 1e-08
DECAY_RATE = 0.01
RATE_QKV = 0.03
RATE_PROJ = 0.3
RATE_UP = 0.03
RATE_DOWN = 0.02
RATE_VECTOR = 0.3
VMEM_BYTES = 60 * 2**20

GATHER_UNITS = ((0, 0), (0, 1), (0, 2), (1, 0), (2, 0), (3, 0), (2, 1), (3, 1))
REDUCE_UNITS = ((3, 0), (2, 0), (3, 1), (2, 1), (1, 0), (0, 0), (0, 1), (0, 2))


def at(start, size, multiple=128):
    return pl.ds(pl.multiple_of(start, multiple), size)


def mm(a, b):
    return jnp.dot(a, b, preferred_element_type=F32)


def mm_lt(a, b):
    return lax.dot_general(a, b, (((0,), (0,)), ((), ())), preferred_element_type=F32)


def mm_rt(a, b):
    return lax.dot_general(a, b, (((1,), (1,)), ((), ())), preferred_element_type=F32)


def piece(unit, full, r, c):
    kind, k = unit
    if kind == 0:
        return full[0].at[k, at(r * BLK, BLK), at(c * HALF, HALF)]
    if kind == 1:
        return full[1].at[at(c * HALF, HALF), at(r * BLK, BLK)]
    if kind == 2:
        return full[2].at[at(r * BLK, BLK), at(c * 2 * HID + k * HID, HID)]
    return full[3].at[at(c * 2 * HID + k * HID, HID), at(r * BLK, BLK)]


def own_piece(unit, own):
    kind, k = unit
    if kind == 0:
        return own[0].at[k]
    if kind == 1:
        return own[1]
    if kind == 2:
        return own[2].at[:, pl.ds(k * HID, HID)]
    return own[3].at[pl.ds(k * HID, HID), :]


def column(unit, full, c):
    kind, k = unit
    if kind == 0:
        return full[0].at[k, :, at(c * HALF, HALF)]
    if kind == 1:
        return full[1].at[at(c * HALF, HALF), :]
    if kind == 2:
        return full[2].at[:, at(c * 2 * HID + k * HID, HID)]
    return full[3].at[at(c * 2 * HID + k * HID, HID), :]


def column_shape(unit):
    return ((D, HALF), (HALF, D), (D, HID), (HID, D))[unit[0]]


def piece_shape(unit):
    return ((BLK, HALF), (HALF, BLK), (BLK, HID), (HID, BLK))[unit[0]]


def row_part(unit, col_ref, r):
    if unit[0] in (0, 2):
        return col_ref.at[at(r * BLK, BLK), :]
    return col_ref.at[:, at(r * BLK, BLK)]


def remote(src, dst, send, recv, **where):
    return pltpu.make_async_remote_copy(
        src_ref=src, dst_ref=dst, send_sem=send, recv_sem=recv, device_id=where, device_id_type=MESH
    )


def position():
    return lax.axis_index("row"), lax.axis_index("col")


def flip(r, bit):
    if bit == 1:
        return r + 1 - 2 * lax.rem(r, 2)
    if bit == 2:
        return lax.rem(r + 2, 4)
    return 3 - r


def greet(dp_count):
    r, c = position()
    barrier = pltpu.get_barrier_semaphore()
    peers = [{"col": 1 - c}, {"row": flip(r, 1)}, {"row": flip(r, 2)}]
    if dp_count:
        z = lax.axis_index("dp")
        peers += [{"dp": lax.rem(z + k, dp_count)} for k in range(1, dp_count)]
    for peer in peers:
        pl.semaphore_signal(barrier, inc=1, device_id=peer, device_id_type=MESH)
    pl.semaphore_wait(barrier, len(peers))


def gather_kernel(
    tok, cot, qkv, proj, up, down, vec,
    x_out, ct_out, qkv_out, proj_out, up_out, down_out, vec_out,
    own_qkv, own_proj, own_up, own_down, send, recv, send_in, recv_in,
):
    r, c = position()
    sib = 1 - c
    full = (qkv_out, proj_out, up_out, down_out)
    own = (own_qkv, own_proj, own_up, own_down)
    for src, dst in zip((qkv, proj, up, down), own):
        dst[...] = src[...].astype(BF)
    greet(0)
    started = []

    def go(copy):
        copy.start()
        started.append(copy)
        return copy

    ins = []
    for i, (src, dst) in enumerate(((tok, x_out), (cot, ct_out))):
        ins.append(go(remote(src.at[at(sib * SEQ, SEQ), :], dst.at[:, at(c * HALF, HALF)],
                             send_in.at[i], recv_in.at[i], col=sib)))
    ins.append(go(remote(vec, vec_out.at[c], send_in.at[2], recv_in.at[2], col=sib)))
    first = []
    for u, unit in enumerate(GATHER_UNITS):
        src, dst = own_piece(unit, own), piece(unit, full, r, c)
        first.append([
            go(remote(src, dst, send.at[u, 0], recv.at[u, 0], row=flip(r, 1))),
            go(remote(src, dst, send.at[u, 1], recv.at[u, 1], row=flip(r, 2))),
            go(remote(src, dst, send.at[u, 3], recv.at[u, 3], col=sib)),
        ])
    for src, dst in ((tok, x_out), (cot, ct_out)):
        dst[:, at(c * HALF, HALF)] = src[at(c * SEQ, SEQ), :]
    vec_out[c] = vec[...]
    for unit in GATHER_UNITS:
        piece(unit, full, r, c)[...] = own_piece(unit, own)[...]
    to_sib, across = [], []
    for u, unit in enumerate(GATHER_UNITS):
        for k, bit in ((0, 1), (1, 2)):
            first[u][k].wait_recv()
            block = piece(unit, full, flip(r, bit), c)
            if k == u % 2:
                across.append(go(remote(block, block, send.at[u, 2], recv.at[u, 2], row=flip(r, 3 - bit))))
            to_sib.append(go(remote(block, block, send.at[u, 4 + k], recv.at[u, 4 + k], col=sib)))
        if u >= 1:
            v = u - 1
            across[v].wait_recv()
            block = piece(GATHER_UNITS[v], full, flip(r, 3), c)
            to_sib.append(go(remote(block, block, send.at[v, 6], recv.at[v, 6], col=sib)))
    v = len(GATHER_UNITS) - 1
    across[v].wait_recv()
    block = piece(GATHER_UNITS[v], full, flip(r, 3), c)
    to_sib.append(go(remote(block, block, send.at[v, 6], recv.at[v, 6], col=sib)))
    for copy in ins:
        copy.wait_recv()
    for u in range(len(GATHER_UNITS)):
        first[u][2].wait_recv()
    for copy in to_sib:
        copy.wait_recv()
    for copy in started:
        copy.wait_send()


def norm_forward(total):
    mean = jnp.mean(total, -1, keepdims=True)
    centered = total - mean
    scale = lax.rsqrt(jnp.mean(centered * centered, -1, keepdims=True) + NORM_EPS)
    return centered * scale, scale


def norm_back(grad, normed, scale, gain):
    scaled = grad * gain
    return scale * (
        scaled - jnp.mean(scaled, -1, keepdims=True) - normed * jnp.mean(scaled * normed, -1, keepdims=True)
    )


def layer_kernel(
    x_ref, ct_ref, qkv, proj, up, down, vec,
    bo_ref, ig_ref, dqkv, dproj, dup, ddown, vg,
    q_s, k_s, v_s, p_s, a_s, u_s, gp_s, h1_s, n1_s, da_s, dq_s, dk_s, dv_s,
):
    def row(i):
        return jnp.concatenate([vec[0, i:i + 1, :], vec[1, i:i + 1, :]], 1)

    def put_row(i, value):
        vg[0, i:i + 1, :] = value[:, :HALF]
        vg[1, i:i + 1, :] = value[:, HALF:]

    def col_sum(value):
        return jnp.sum(value, 0, keepdims=True)

    x = x_ref[...]
    scaling = HEAD_DIM ** (-0.5)
    q_s[...] = (mm(x, qkv[0]) + row(0)).astype(BF)
    k_s[...] = mm(x, qkv[1]).astype(BF)
    v_s[...] = (mm(x, qkv[2]) + row(1)).astype(BF)
    for h in range(HEADS):
        cols = slice(h * HEAD_DIM, (h + 1) * HEAD_DIM)
        s = mm_rt(q_s[:, cols], k_s[:, cols]) * scaling
        e = jnp.exp(s - jnp.max(s, -1, keepdims=True))
        p = e * (1.0 / jnp.sum(e, -1, keepdims=True))
        p_s[h] = p
        a_s[:, cols] = mm(p.astype(BF), v_s[:, cols]).astype(BF)
    n1, scale1 = norm_forward(x.astype(F32) + mm(a_s[...], proj[...]) + row(2))
    n1_s[...] = n1
    h1 = n1 * row(4) + row(5)
    h1b = h1.astype(BF)
    h1_s[...] = h1b
    acc = h1 + row(3)
    for j in range(4):
        c, k = j // 2, 2 * (j % 2)
        bias = jnp.concatenate([vec[c, 8 + k:9 + k, :], vec[c, 9 + k:10 + k, :]], 1)
        cols = slice(j * HID, (j + 1) * HID)
        z = mm(h1b, up[:, cols]) + bias
        half = 0.5 + 0.5 * lax.erf(z * 0.7071067811865476)
        u = (z * half).astype(BF)
        u_s[:, cols] = u
        gp_s[:, cols] = half + z * (0.3989422804014327 * jnp.exp(-0.5 * z * z))
        acc = acc + mm(u, down[cols, :])
    n2, scale2 = norm_forward(acc)
    bo_ref[...] = (n2 * row(6) + row(7)).astype(BF)
    dy = ct_ref[...].astype(F32)
    put_row(6, col_sum(dy * n2))
    put_row(7, col_sum(dy))
    dr2 = norm_back(dy, n2, scale2, row(6))
    put_row(3, col_sum(dr2))
    g2 = dr2.astype(BF)
    acc = dr2
    for j in (0, 2, 1, 3):
        c, k = j // 2, 2 * (j % 2)
        cols = slice(j * HID, (j + 1) * HID)
        ddown[cols, :] = mm_lt(u_s[:, cols], g2).astype(BF)
        dz = (mm_rt(g2, down[cols, :]) * gp_s[:, cols]).astype(BF)
        db = col_sum(dz.astype(F32))
        vg[c, 8 + k:9 + k, :] = db[:, :HALF]
        vg[c, 9 + k:10 + k, :] = db[:, HALF:]
        dup[:, cols] = mm_lt(h1_s[...], dz).astype(BF)
        acc = acc + mm_rt(dz, up[:, cols])
    n1 = n1_s[...]
    put_row(4, col_sum(acc * n1))
    put_row(5, col_sum(acc))
    dr1 = norm_back(acc, n1, scale1, row(4))
    put_row(2, col_sum(dr1))
    ig_ref[...] = dr1
    g1 = dr1.astype(BF)
    dproj[...] = mm_lt(a_s[...], g1).astype(BF)
    da_s[...] = mm_rt(g1, proj[...]).astype(BF)
    for h in range(HEADS):
        cols = slice(h * HEAD_DIM, (h + 1) * HEAD_DIM)
        da = da_s[:, cols]
        p = p_s[h]
        dp = mm_rt(da, v_s[:, cols])
        ds = (p * (dp - jnp.sum(p * dp, -1, keepdims=True))).astype(BF)
        dq_s[:, cols] = (mm(ds, k_s[:, cols]) * scaling).astype(BF)
        dk_s[:, cols] = (mm_lt(ds, q_s[:, cols]) * scaling).astype(BF)
        dv_s[:, cols] = mm_lt(p.astype(BF), da).astype(BF)
    dq, dk, dv = dq_s[...], dk_s[...], dv_s[...]
    put_row(0, col_sum(dq.astype(F32)))
    put_row(1, col_sum(dv.astype(F32)))
    dqkv[0] = mm_lt(x, dq).astype(BF)
    dqkv[1] = mm_lt(x, dk).astype(BF)
    dqkv[2] = mm_lt(x, dv).astype(BF)
    ig_ref[...] = ig_ref[...] + mm_rt(dq, qkv[0]) + mm_rt(dk, qkv[1]) + mm_rt(dv, qkv[2])


def reduce_kernel(dp_count, *refs):
    n = len(REDUCE_UNITS)
    bo, ig, dqkv, dproj, dup, ddown, vg = refs[:7]
    bo_out, ig_out, gqkv, gproj, gup, gdown, gvec = refs[7:14]
    rest = list(refs[14:])
    sib_buf, sums, buf_a, buf_b, send_b, zsrc, zbuf = (
        [rest.pop(0) for _ in range(n)] for _ in range(7)
    )
    vsum, vbuf, send, recv, send_v, recv_v = rest
    full, outs = (dqkv, dproj, dup, ddown), (gqkv, gproj, gup, gdown)
    r, c = position()
    sib = 1 - c
    z = lax.axis_index("dp") if dp_count else None
    greet(dp_count)
    started = []

    def go(copy):
        copy.start()
        started.append(copy)
        return copy

    flying = {}

    def wait(key):
        for copy in flying.pop(key):
            copy.wait_recv()

    def add(*views):
        total = views[0][...].astype(F32)
        for view in views[1:]:
            total = total + view[...].astype(F32)
        return total

    def quarter(unit, ref, k):
        depth = piece_shape(unit)[0] // dp_count
        return ref.at[at(k * depth, depth, 16), :]

    def phase(u, step):
        unit = REDUCE_UNITS[u]
        a, b = (1, 2) if u % 2 == 0 else (2, 1)
        if step == 0:
            flying[u] = [go(remote(column(unit, full, sib), sib_buf[u], send.at[u, 0], recv.at[u, 0], col=sib))]
        elif step == 1:
            wait(u)
            sums[u][...] = add(column(unit, full, c), sib_buf[u]).astype(BF)
            peer = flip(r, a)
            flying[u] = [
                go(remote(row_part(unit, sums[u], who), buf_a[u].at[i], send.at[u, 1 + i], recv.at[u, 1 + i], row=peer))
                for i, who in ((1, flip(r, 3)), (0, peer))
            ]
        elif step == 2:
            wait(u)
            send_b[u][...] = add(row_part(unit, sums[u], flip(r, b)), buf_a[u].at[1]).astype(BF)
            flying[u] = [go(remote(send_b[u], buf_b[u], send.at[u, 3], recv.at[u, 3], row=flip(r, b)))]
        elif step == 3:
            wait(u)
            total = add(row_part(unit, sums[u], r), buf_a[u].at[0], buf_b[u]).astype(BF)
            if not dp_count:
                own_piece(unit, outs)[...] = total
                return
            zsrc[u][...] = total
            flying[u] = []
            for k in range(1, dp_count):
                to = lax.rem(z + k, dp_count)
                flying[u].append(go(remote(
                    quarter(unit, zsrc[u], to), zbuf[u].at[k - 1], send.at[u, 3 + k], recv.at[u, 3 + k], dp=to)))
        elif step == 4:
            if not dp_count:
                return
            wait(u)
            mine = quarter(unit, own_piece(unit, outs), z)
            mine[...] = add(quarter(unit, zsrc[u], z), *[zbuf[u].at[k] for k in range(dp_count - 1)]).astype(BF)
            flying[u] = []
            for k in range(1, dp_count):
                to = lax.rem(z + k, dp_count)
                flying[u].append(go(remote(
                    mine, mine, send.at[u, 2 + dp_count + k], recv.at[u, 2 + dp_count + k], dp=to)))
        else:
            if dp_count:
                wait(u)

    phase(0, 0)
    phase(1, 0)
    back = [
        go(remote(src.at[:, at(sib * HALF, HALF)], dst.at[at(c * SEQ, SEQ), :], send_v.at[i], recv_v.at[i], col=sib))
        for i, (src, dst) in enumerate(((bo, bo_out), (ig, ig_out)))
    ]
    for src, dst in ((bo, bo_out), (ig, ig_out)):
        dst[at(c * SEQ, SEQ), :] = src[:, at(c * HALF, HALF)]

    def vec_step(step):
        if step == 0:
            flying["v"] = [go(remote(vg.at[sib], vbuf.at[0], send_v.at[2], recv_v.at[2], col=sib))]
        elif step == 1:
            wait("v")
            vsum[0] = vg[c] + vbuf[0]
            flying["v"] = [go(remote(vsum.at[0], vbuf.at[1], send_v.at[3], recv_v.at[3], row=flip(r, 1)))]
        elif step == 2:
            wait("v")
            vsum[1] = vsum[0] + vbuf[1]
            flying["v"] = [go(remote(vsum.at[1], vbuf.at[2], send_v.at[4], recv_v.at[4], row=flip(r, 2)))]
        elif step == 3:
            wait("v")
            total = vsum[1] + vbuf[2]
            if not dp_count:
                gvec[...] = total
                return
            vsum[2] = total
            flying["v"] = [
                go(remote(vsum.at[2], vbuf.at[2 + k], send_v.at[4 + k], recv_v.at[4 + k],
                          dp=lax.rem(z + k, dp_count)))
                for k in range(1, dp_count)
            ]
        elif step == 4 and dp_count:
            wait("v")
            parts = [vsum[2]] + [vbuf[2 + k] for k in range(1, dp_count)]
            total = jnp.zeros_like(parts[0])
            for owner in range(dp_count):
                for k, part in enumerate(parts):
                    total = total + jnp.where(lax.rem(z + dp_count - k, dp_count) == owner, part, 0.0)
            gvec[...] = total

    for tick in range(1, n + 6):
        for step in (5, 4, 3, 2, 1):
            u = tick - step
            if 0 <= u < n:
                phase(u, step)
        if tick + 1 < n:
            phase(tick + 1, 0)
        if tick <= 5:
            vec_step(tick - 1)
    for copy in back:
        copy.wait_recv()
    for copy in started:
        copy.wait_send()


def adam_step(weight, mean_old, square_old, gradient, step_rate, decay_rate):
    mean_new = BETA_ONE * mean_old + (1.0 - BETA_ONE) * gradient
    square_new = BETA_TWO * square_old + (1.0 - BETA_TWO) * gradient * gradient
    mean_hat = mean_new / (1.0 - BETA_ONE**STEP)
    square_hat = square_new / (1.0 - BETA_TWO**STEP)
    weight_new = weight - step_rate * (
        mean_hat / (jnp.sqrt(square_hat) + ADAM_EPS) + decay_rate * weight
    )
    return (weight_new, mean_new, square_new)


def shape(dims, dtype):
    return jax.ShapeDtypeStruct(dims, dtype)


def call(kernel, ins, outs, scratch, collective_id=None):
    vmem = pl.BlockSpec(memory_space=pltpu.VMEM)
    extra = {} if collective_id is None else dict(collective_id=collective_id, has_side_effects=True)
    return pl.pallas_call(
        kernel,
        out_shape=outs,
        in_specs=[vmem] * len(ins),
        out_specs=[vmem] * len(outs),
        scratch_shapes=scratch,
        compiler_params=pltpu.CompilerParams(vmem_limit_bytes=VMEM_BYTES, **extra),
    )(*ins)


FULL = ((3, D, D), (D, D), (D, FF), (FF, D))
OWN = ((3, BLK, HALF), (HALF, BLK), (BLK, FF // 2), (FF // 2, BLK))


def body(
    dp_size,
    tokens, cotangent, qkv_weight, proj_weight, up_weight, down_weight, vectors,
    qkv_mean, qkv_square, proj_mean, proj_square, up_mean, up_square,
    down_mean, down_square, vector_mean, vector_square,
):
    dma = pltpu.SemaphoreType.DMA
    vm = pltpu.VMEM
    n = len(GATHER_UNITS)
    gathered = call(
        gather_kernel,
        (tokens, cotangent, qkv_weight, proj_weight, up_weight, down_weight, vectors),
        [shape((SEQ, D), BF)] * 2 + [shape(s, BF) for s in FULL] + [shape((2, 12, HALF), F32)],
        [vm(s, BF) for s in OWN] + [dma((n, 7)), dma((n, 7)), dma((3,)), dma((3,))],
        collective_id=0,
    )
    sq = vm((SEQ, D), BF)
    partial = call(
        layer_kernel,
        gathered,
        [shape((SEQ, D), BF), shape((SEQ, D), F32)] + [shape(s, BF) for s in FULL] + [shape((2, 12, HALF), F32)],
        [sq, sq, sq, vm((HEADS, SEQ, SEQ), F32), sq, vm((SEQ, FF), BF), vm((SEQ, FF), F32), sq,
         vm((SEQ, D), F32), sq, sq, sq, sq],
    )
    dp_count = dp_size if dp_size == 4 else 0
    zn = dp_count or 4
    units = REDUCE_UNITS
    pieces = [piece_shape(u) for u in units]
    reduced = call(
        functools.partial(reduce_kernel, dp_count),
        partial,
        [shape((2 * SEQ, HALF), BF), shape((2 * SEQ, HALF), F32)] + [shape(s, BF) for s in OWN]
        + [shape((12, HALF), F32)],
        [vm(column_shape(u), BF) for u in units] + [vm(column_shape(u), BF) for u in units]
        + [vm((2,) + s, BF) for s in pieces] + [vm(s, BF) for s in pieces] + [vm(s, BF) for s in pieces]
        + [vm(s, BF) for s in pieces] + [vm((zn - 1, s[0] // zn, s[1]), BF) for s in pieces]
        + [vm((3, 12, HALF), F32), vm((2 + zn, 12, HALF), F32),
           dma((n, 3 + 2 * zn)), dma((n, 3 + 2 * zn)), dma((4 + zn,)), dma((4 + zn,))],
        collective_id=1,
    )
    output, input_grad, grads, vector_grad = reduced[0], reduced[1], reduced[2:6], reduced[6]
    grads = [g.astype(F32) for g in grads]
    if not dp_count:
        grads = [lax.psum(g, "dp") for g in grads]
        vector_grad = lax.psum(vector_grad, "dp")
    return (
        output,
        input_grad,
        *adam_step(qkv_weight, qkv_mean, qkv_square, grads[0], RATE_QKV, DECAY_RATE),
        *adam_step(proj_weight, proj_mean, proj_square, grads[1], RATE_PROJ, DECAY_RATE),
        *adam_step(up_weight, up_mean, up_square, grads[2], RATE_UP, DECAY_RATE),
        *adam_step(down_weight, down_mean, down_square, grads[3], RATE_DOWN, DECAY_RATE),
        *adam_step(vectors, vector_mean, vector_square, vector_grad, RATE_VECTOR, 0.0),
        vector_grad,
    )


def solution(mesh):
    tokens = P(("dp", "row"), "col")
    qkv, proj, up, down, vec = P(None, "row", "col"), P("col", "row"), P("row", "col"), P("col", "row"), P(None, "col")
    return jax.shard_map(
        functools.partial(body, mesh.shape["dp"]),
        mesh=mesh,
        in_specs=(tokens, tokens, qkv, proj, up, down, vec, qkv, qkv, proj, proj, up, up, down, down, vec, vec),
        out_specs=(tokens, tokens) + (qkv,) * 3 + (proj,) * 3 + (up,) * 3 + (down,) * 3 + (vec,) * 4,
        check_vma=False,
    )
```

```python
import functools

import jax
import jax.numpy as jnp
from jax import lax
from jax.experimental import pallas as pl
from jax.experimental.pallas import tpu as pltpu
from jax.sharding import PartitionSpec as P

MESH = pl.DeviceIdType.MESH
BF = jnp.bfloat16
F32 = jnp.float32

D = 512
HEADS = 8
HEAD_DIM = 64
FF = 2048
SEQ = 512
STEP = 10
ROWS = 4
HALF = D // 2
BLK = D // ROWS
HID = 512

NORM_EPS = 1e-05
BETA_ONE = 0.9
BETA_TWO = 0.999
ADAM_EPS = 1e-08
DECAY_RATE = 0.01
RATE_QKV = 0.03
RATE_PROJ = 0.3
RATE_UP = 0.03
RATE_DOWN = 0.02
RATE_VECTOR = 0.3
VMEM_BYTES = 60 * 2**20

GATHER_UNITS = ((0, 0), (0, 1), (0, 2), (1, 0), (2, 0), (3, 0), (2, 1), (3, 1))
REDUCE_UNITS = ((3, 0), (2, 0), (3, 1), (2, 1), (1, 0), (0, 0), (0, 1), (0, 2))


def at(start, size, multiple=128):
    return pl.ds(pl.multiple_of(start, multiple), size)


def mm(a, b):
    return jnp.dot(a, b, preferred_element_type=F32)


def mm_lt(a, b):
    return lax.dot_general(a, b, (((0,), (0,)), ((), ())), preferred_element_type=F32)


def mm_rt(a, b):
    return lax.dot_general(a, b, (((1,), (1,)), ((), ())), preferred_element_type=F32)


def piece(unit, full, r, c):
    kind, k = unit
    if kind == 0:
        return full[0].at[k, at(r * BLK, BLK), at(c * HALF, HALF)]
    if kind == 1:
        return full[1].at[at(c * HALF, HALF), at(r * BLK, BLK)]
    if kind == 2:
        return full[2].at[at(r * BLK, BLK), at(c * 2 * HID + k * HID, HID)]
    return full[3].at[at(c * 2 * HID + k * HID, HID), at(r * BLK, BLK)]


def own_piece(unit, own):
    kind, k = unit
    if kind == 0:
        return own[0].at[k]
    if kind == 1:
        return own[1]
    if kind == 2:
        return own[2].at[:, pl.ds(k * HID, HID)]
    return own[3].at[pl.ds(k * HID, HID), :]


def column(unit, full, c):
    kind, k = unit
    if kind == 0:
        return full[0].at[k, :, at(c * HALF, HALF)]
    if kind == 1:
        return full[1].at[at(c * HALF, HALF), :]
    if kind == 2:
        return full[2].at[:, at(c * 2 * HID + k * HID, HID)]
    return full[3].at[at(c * 2 * HID + k * HID, HID), :]


def column_shape(unit):
    return ((D, HALF), (HALF, D), (D, HID), (HID, D))[unit[0]]


def piece_shape(unit):
    return ((BLK, HALF), (HALF, BLK), (BLK, HID), (HID, BLK))[unit[0]]


def row_part(unit, col_ref, r):
    if unit[0] in (0, 2):
        return col_ref.at[at(r * BLK, BLK), :]
    return col_ref.at[:, at(r * BLK, BLK)]


def remote(src, dst, send, recv, **where):
    return pltpu.make_async_remote_copy(
        src_ref=src, dst_ref=dst, send_sem=send, recv_sem=recv, device_id=where, device_id_type=MESH
    )


def position():
    return lax.axis_index("row"), lax.axis_index("col")


def flip(r, bit):
    if bit == 1:
        return r + 1 - 2 * lax.rem(r, 2)
    if bit == 2:
        return lax.rem(r + 2, 4)
    return 3 - r


def greet(dp_count):
    r, c = position()
    barrier = pltpu.get_barrier_semaphore()
    peers = [{"col": 1 - c}, {"row": flip(r, 1)}, {"row": flip(r, 2)}]
    if dp_count:
        z = lax.axis_index("dp")
        peers += [{"dp": lax.rem(z + k, dp_count)} for k in range(1, dp_count)]
    for peer in peers:
        pl.semaphore_signal(barrier, inc=1, device_id=peer, device_id_type=MESH)
    pl.semaphore_wait(barrier, len(peers))


def norm_forward(total):
    mean = jnp.mean(total, -1, keepdims=True)
    centered = total - mean
    scale = lax.rsqrt(jnp.mean(centered * centered, -1, keepdims=True) + NORM_EPS)
    return centered * scale, scale


def norm_back(grad, normed, scale, gain):
    scaled = grad * gain
    return scale * (
        scaled - jnp.mean(scaled, -1, keepdims=True) - normed * jnp.mean(scaled * normed, -1, keepdims=True)
    )


def col_sum(value):
    return jnp.sum(value, 0, keepdims=True)


def kernel(dp_count, *refs):
    n = len(REDUCE_UNITS)
    refs = list(refs)

    def take(count):
        out = refs[:count]
        del refs[:count]
        return out

    tok, cot, qkv_in, proj_in, up_in, down_in, vec_in = take(7)
    bo_out, ig_out, gqkv, gproj, gup, gdown, gvec = take(7)
    x_ref, ct_ref, qkv, proj, up, down, vec = take(7)
    own = take(4)
    bo, ig, dqkv, dproj, dup, ddown, vg = take(7)
    q_s, k_s, v_s, p_s, a_s, u_s, gp_s, h1_s, n1_s, da_s, dq_s, dk_s, dv_s = take(13)
    sib_buf, sums, buf_a, buf_b, send_b, zsrc, zbuf = (take(n) for _ in range(7))
    vsum, vbuf, send_in, recv_in, send_g, recv_g, send, recv, send_v, recv_v = take(10)
    full = (qkv, proj, up, down)
    grads, outs = (dqkv, dproj, dup, ddown), (gqkv, gproj, gup, gdown)
    r, c = position()
    sib = 1 - c
    z = lax.axis_index("dp") if dp_count else None
    started, started_end, started_mid = [], [], []
    if dp_count:
        middle = jnp.logical_or(z == 1, z == 2)
        end = jnp.logical_not(middle)

    def go(copy, kept=started):
        copy.start()
        kept.append(copy)
        return copy

    for src, dst in zip((qkv_in, proj_in, up_in, down_in), own):
        dst[...] = src[...].astype(BF)
    greet(dp_count)
    first, across, to_sib = {}, {}, {}

    def issue(u):
        unit = GATHER_UNITS[u]
        src, dst = own_piece(unit, own), piece(unit, full, r, c)
        first[u] = [
            go(remote(src, dst, send_g.at[u, 0], recv_g.at[u, 0], row=flip(r, 1))),
            go(remote(src, dst, send_g.at[u, 1], recv_g.at[u, 1], row=flip(r, 2))),
        ]
        to_sib[u] = [go(remote(src, dst, send_g.at[u, 3], recv_g.at[u, 3], col=sib))]

    def near(u):
        unit = GATHER_UNITS[u]
        for k, bit in ((0, 1), (1, 2)):
            first[u][k].wait_recv()
            block = piece(unit, full, flip(r, bit), c)
            if k == u % 2:
                across[u] = go(remote(block, block, send_g.at[u, 2], recv_g.at[u, 2], row=flip(r, 3 - bit)))
            to_sib[u].append(go(remote(block, block, send_g.at[u, 4 + k], recv_g.at[u, 4 + k], col=sib)))

    def far(u):
        across[u].wait_recv()
        block = piece(GATHER_UNITS[u], full, flip(r, 3), c)
        to_sib[u].append(go(remote(block, block, send_g.at[u, 6], recv_g.at[u, 6], col=sib)))

    def whole(u):
        for copy in to_sib[u]:
            copy.wait_recv()

    ins = [
        go(remote(src.at[at(sib * SEQ, SEQ), :], dst.at[:, at(c * HALF, HALF)], send_in.at[i], recv_in.at[i], col=sib))
        for i, (src, dst) in enumerate(((tok, x_ref), (cot, ct_ref)))
    ]
    ins.append(go(remote(vec_in, vec.at[c], send_in.at[2], recv_in.at[2], col=sib)))
    for u in range(5):
        issue(u)
    for src, dst in ((tok, x_ref), (cot, ct_ref)):
        dst[:, at(c * HALF, HALF)] = src[at(c * SEQ, SEQ), :]
    vec[c] = vec_in[...]
    for unit in GATHER_UNITS:
        piece(unit, full, r, c)[...] = own_piece(unit, own)[...]

    flying = {}

    def wait(key):
        for copy in flying.pop(key):
            copy.wait_recv()

    def add(*views):
        total = views[0][...].astype(F32)
        for view in views[1:]:
            total = total + view[...].astype(F32)
        return total

    def phase(u, step):
        unit = REDUCE_UNITS[u]
        a, b = (1, 2) if u % 2 == 0 else (2, 1)
        out = own_piece(unit, outs)
        if step == 0:
            flying[u] = [go(remote(column(unit, grads, sib), sib_buf[u], send.at[u, 0], recv.at[u, 0], col=sib))]
        elif step == 1:
            wait(u)
            sums[u][...] = add(column(unit, grads, c), sib_buf[u]).astype(BF)
            peer = flip(r, a)
            flying[u] = [
                go(remote(row_part(unit, sums[u], who), buf_a[u].at[i], send.at[u, 1 + i], recv.at[u, 1 + i], row=peer))
                for i, who in ((1, flip(r, 3)), (0, peer))
            ]
        elif step == 2:
            wait(u)
            send_b[u][...] = add(row_part(unit, sums[u], flip(r, b)), buf_a[u].at[1]).astype(BF)
            flying[u] = [go(remote(send_b[u], buf_b[u], send.at[u, 3], recv.at[u, 3], row=flip(r, b)))]
        elif step == 3:
            wait(u)
            total = add(row_part(unit, sums[u], r), buf_a[u].at[0], buf_b[u]).astype(BF)
            if not dp_count:
                out[...] = total
                return
            zsrc[u][...] = total
            side = remote(zsrc[u], zbuf[u].at[0], send.at[u, 4], recv.at[u, 4], dp=flip(z, 1))
            inner = remote(zsrc[u], zbuf[u].at[1], send.at[u, 5], recv.at[u, 5], dp=3 - z)
            back = remote(out, out, send.at[u, 6], recv.at[u, 6], dp=flip(z, 1))
            flying[u] = (side, inner, back)

            @pl.when(end)
            def _():
                go(side, started_end)
        elif dp_count and step == 4:
            side, inner, back = flying[u]

            @pl.when(middle)
            def _():
                side.wait_recv()
                zsrc[u][...] = add(zsrc[u], zbuf[u].at[0]).astype(BF)
                go(inner, started_mid)
        elif dp_count and step == 5:
            side, inner, back = flying[u]

            @pl.when(middle)
            def _():
                inner.wait_recv()
                out[...] = add(zsrc[u], zbuf[u].at[1]).astype(BF)
                go(back, started_mid)
        elif dp_count:
            side, inner, back = flying[u]

            @pl.when(end)
            def _():
                back.wait_recv()

    def vec_step(step):
        if step == 0:
            flying["v"] = [go(remote(vg.at[sib], vbuf.at[0], send_v.at[2], recv_v.at[2], col=sib))]
        elif step == 1:
            wait("v")
            vsum[0] = vg[c] + vbuf[0]
            flying["v"] = [go(remote(vsum.at[0], vbuf.at[1], send_v.at[3], recv_v.at[3], row=flip(r, 1)))]
        elif step == 2:
            wait("v")
            vsum[1] = vsum[0] + vbuf[1]
            flying["v"] = [go(remote(vsum.at[1], vbuf.at[2], send_v.at[4], recv_v.at[4], row=flip(r, 2)))]
        elif step == 3:
            wait("v")
            total = vsum[1] + vbuf[2]
            if not dp_count:
                gvec[...] = total
                return
            vsum[2] = total
            flying["v"] = [
                go(remote(vsum.at[2], vbuf.at[2 + k], send_v.at[4 + k], recv_v.at[4 + k],
                          dp=lax.rem(z + k, dp_count)))
                for k in range(1, dp_count)
            ]
        elif step == 4 and dp_count:
            wait("v")
            parts = [vsum[2]] + [vbuf[2 + k] for k in range(1, dp_count)]
            total = jnp.zeros_like(parts[0])
            for owner in range(dp_count):
                for k, part in enumerate(parts):
                    total = total + jnp.where(lax.rem(z + dp_count - k, dp_count) == owner, part, 0.0)
            gvec[...] = total

    def tick(t):
        for step in (6, 5, 4, 3, 2, 1):
            if 0 <= t - step < n:
                phase(t - step, step)

    def give_back(i, src, dst):
        copy = go(remote(src.at[:, at(sib * HALF, HALF)], dst.at[at(c * SEQ, SEQ), :],
                         send_v.at[i], recv_v.at[i], col=sib))
        dst[at(c * SEQ, SEQ), :] = src[:, at(c * HALF, HALF)]
        return copy

    def row(i):
        return jnp.concatenate([vec[0, i:i + 1, :], vec[1, i:i + 1, :]], 1)

    def put_row(i, value):
        vg[0, i:i + 1, :] = value[:, :HALF]
        vg[1, i:i + 1, :] = value[:, HALF:]

    near(0)
    issue(5)
    near(1)
    far(0)
    issue(6)
    near(2)
    far(1)
    issue(7)
    for copy in ins:
        copy.wait_recv()
    whole(0)
    scaling = HEAD_DIM ** (-0.5)
    q_s[...] = (mm(x_ref[...], qkv[0]) + row(0)).astype(BF)
    far(2)
    whole(1)
    k_s[...] = mm(x_ref[...], qkv[1]).astype(BF)
    near(3)
    whole(2)
    v_s[...] = (mm(x_ref[...], qkv[2]) + row(1)).astype(BF)
    beside = {0: ((far, 3),), 1: ((near, 4),), 3: ((near, 5), (far, 4)), 5: ((near, 6), (far, 5)),
              7: ((near, 7), (far, 6))}
    for h in range(HEADS):
        cols = slice(h * HEAD_DIM, (h + 1) * HEAD_DIM)
        s = mm_rt(q_s[:, cols], k_s[:, cols]) * scaling
        e = jnp.exp(s - jnp.max(s, -1, keepdims=True))
        p = e * (1.0 / jnp.sum(e, -1, keepdims=True))
        p_s[h] = p
        a_s[:, cols] = mm(p.astype(BF), v_s[:, cols]).astype(BF)
        for act, u in beside.get(h, ()):
            act(u)
    whole(3)
    n1, scale1 = norm_forward(x_ref[...].astype(F32) + mm(a_s[...], proj[...]) + row(2))
    n1_s[...] = n1
    h1 = n1 * row(4) + row(5)
    h1_s[...] = h1.astype(BF)
    far(7)
    acc = h1 + row(3)
    for j in (0, 2, 1, 3):
        if j < 2:
            whole(4 + 2 * j)
            whole(5 + 2 * j)
        c_of, k = j // 2, 2 * (j % 2)
        bias = jnp.concatenate([vec[c_of, 8 + k:9 + k, :], vec[c_of, 9 + k:10 + k, :]], 1)
        cols = slice(j * HID, (j + 1) * HID)
        pre = mm(h1_s[...], up[:, cols]) + bias
        half = 0.5 + 0.5 * lax.erf(pre * 0.7071067811865476)
        u = (pre * half).astype(BF)
        u_s[:, cols] = u
        gp_s[:, cols] = half + pre * (0.3989422804014327 * jnp.exp(-0.5 * pre * pre))
        acc = acc + mm(u, down[cols, :])
    n2, scale2 = norm_forward(acc)
    bo[...] = (n2 * row(6) + row(7)).astype(BF)
    give = [give_back(0, bo, bo_out)]

    dy = ct_ref[...].astype(F32)
    put_row(6, col_sum(dy * n2))
    put_row(7, col_sum(dy))
    dr2 = norm_back(dy, n2, scale2, row(6))
    put_row(3, col_sum(dr2))
    g2 = dr2.astype(BF)
    ig[...] = dr2
    for j in (0, 2, 1, 3):
        c_of, k = j // 2, 2 * (j % 2)
        cols = slice(j * HID, (j + 1) * HID)
        ddown[cols, :] = mm_lt(u_s[:, cols], g2).astype(BF)
        if j >= 2:
            phase(2 * (j - 2), 0)
        dz = (mm_rt(g2, down[cols, :]) * gp_s[:, cols]).astype(BF)
        db = col_sum(dz.astype(F32))
        vg[c_of, 8 + k:9 + k, :] = db[:, :HALF]
        vg[c_of, 9 + k:10 + k, :] = db[:, HALF:]
        dup[:, cols] = mm_lt(h1_s[...], dz).astype(BF)
        if j >= 2:
            phase(2 * (j - 2) + 1, 0)
        if j == 3:
            tick(1)
        ig[...] = ig[...] + mm_rt(dz, up[:, cols])
    tick(2)
    acc = ig[...]
    n1 = n1_s[...]
    put_row(4, col_sum(acc * n1))
    put_row(5, col_sum(acc))
    dr1 = norm_back(acc, n1, scale1, row(4))
    put_row(2, col_sum(dr1))
    ig[...] = dr1
    g1 = dr1.astype(BF)
    dproj[...] = mm_lt(a_s[...], g1).astype(BF)
    phase(4, 0)
    da_s[...] = mm_rt(g1, proj[...]).astype(BF)
    tick(3)
    for h in range(HEADS):
        cols = slice(h * HEAD_DIM, (h + 1) * HEAD_DIM)
        da = da_s[:, cols]
        p = p_s[h]
        dp = mm_rt(da, v_s[:, cols])
        ds = (p * (dp - jnp.sum(p * dp, -1, keepdims=True))).astype(BF)
        dq_s[:, cols] = (mm(ds, k_s[:, cols]) * scaling).astype(BF)
        dk_s[:, cols] = (mm_lt(ds, q_s[:, cols]) * scaling).astype(BF)
        dv_s[:, cols] = mm_lt(p.astype(BF), da).astype(BF)
        if h == 2:
            tick(4)
        if h == 5:
            tick(5)
    for i, (src, weight) in enumerate(((dq_s, 0), (dk_s, 1), (dv_s, 2))):
        grad = src[...]
        dqkv[weight] = mm_lt(x_ref[...], grad).astype(BF)
        phase(5 + i, 0)
        if i != 1:
            put_row(i // 2, col_sum(grad.astype(F32)))
    vec_step(0)
    tick(6)
    ig[...] = ig[...] + mm_rt(dq_s[...], qkv[0]) + mm_rt(dk_s[...], qkv[1]) + mm_rt(dv_s[...], qkv[2])
    give.append(give_back(1, ig, ig_out))
    for t in range(7, n + 7):
        tick(t)
        if t <= 10:
            vec_step(t - 6)
    for copy in give:
        copy.wait_recv()
    for copy in started:
        copy.wait_send()
    if dp_count:
        @pl.when(end)
        def _():
            for copy in started_end:
                copy.wait_send()

        @pl.when(middle)
        def _():
            for copy in started_mid:
                copy.wait_send()


def adam_step(weight, mean_old, square_old, gradient, step_rate, decay_rate):
    mean_new = BETA_ONE * mean_old + (1.0 - BETA_ONE) * gradient
    square_new = BETA_TWO * square_old + (1.0 - BETA_TWO) * gradient * gradient
    mean_hat = mean_new / (1.0 - BETA_ONE**STEP)
    square_hat = square_new / (1.0 - BETA_TWO**STEP)
    weight_new = weight - step_rate * (
        mean_hat / (jnp.sqrt(square_hat) + ADAM_EPS) + decay_rate * weight
    )
    return (weight_new, mean_new, square_new)


def shape(dims, dtype):
    return jax.ShapeDtypeStruct(dims, dtype)


def call(kernel, ins, outs, scratch, collective_id=None):
    vmem = pl.BlockSpec(memory_space=pltpu.VMEM)
    extra = {} if collective_id is None else dict(collective_id=collective_id, has_side_effects=True)
    return pl.pallas_call(
        kernel,
        out_shape=outs,
        in_specs=[vmem] * len(ins),
        out_specs=[vmem] * len(outs),
        scratch_shapes=scratch,
        compiler_params=pltpu.CompilerParams(vmem_limit_bytes=VMEM_BYTES, **extra),
    )(*ins)


FULL = ((3, D, D), (D, D), (D, FF), (FF, D))
OWN = ((3, BLK, HALF), (HALF, BLK), (BLK, FF // 2), (FF // 2, BLK))


def body(
    dp_size,
    tokens, cotangent, qkv_weight, proj_weight, up_weight, down_weight, vectors,
    qkv_mean, qkv_square, proj_mean, proj_square, up_mean, up_square,
    down_mean, down_square, vector_mean, vector_square,
):
    dma, vm = pltpu.SemaphoreType.DMA, pltpu.VMEM
    n = len(REDUCE_UNITS)
    dp_count = dp_size if dp_size == 4 else 0
    pieces = [piece_shape(u) for u in REDUCE_UNITS]
    columns = [column_shape(u) for u in REDUCE_UNITS]
    sq, whole = vm((SEQ, D), BF), [vm(s, BF) for s in FULL]
    reduced = call(
        functools.partial(kernel, dp_count),
        (tokens, cotangent, qkv_weight, proj_weight, up_weight, down_weight, vectors),
        [shape((2 * SEQ, HALF), BF), shape((2 * SEQ, HALF), F32)] + [shape(s, BF) for s in OWN]
        + [shape((12, HALF), F32)],
        [sq, sq] + whole + [vm((2, 12, HALF), F32)]
        + [vm(s, BF) for s in OWN]
        + [sq, vm((SEQ, D), F32)] + whole + [vm((2, 12, HALF), F32)]
        + [sq, sq, sq, vm((HEADS, SEQ, SEQ), F32), sq, vm((SEQ, FF), BF), vm((SEQ, FF), F32), sq,
           vm((SEQ, D), F32), sq, sq, sq, sq]
        + [vm(s, BF) for s in columns] * 2
        + [vm((2,) + s, BF) for s in pieces] + [vm(s, BF) for s in pieces] * 3 + [vm((2,) + s, BF) for s in pieces]
        + [vm((3, 12, HALF), F32), vm((6, 12, HALF), F32),
           dma((3,)), dma((3,)), dma((n, 7)), dma((n, 7)), dma((n, 7)), dma((n, 7)), dma((8,)), dma((8,))],
        collective_id=0,
    )
    output, input_grad, grads, vector_grad = reduced[0], reduced[1], reduced[2:6], reduced[6]
    grads = [g.astype(F32) for g in grads]
    if not dp_count:
        grads = [lax.psum(g, "dp") for g in grads]
        vector_grad = lax.psum(vector_grad, "dp")
    return (
        output,
        input_grad,
        *adam_step(qkv_weight, qkv_mean, qkv_square, grads[0], RATE_QKV, DECAY_RATE),
        *adam_step(proj_weight, proj_mean, proj_square, grads[1], RATE_PROJ, DECAY_RATE),
        *adam_step(up_weight, up_mean, up_square, grads[2], RATE_UP, DECAY_RATE),
        *adam_step(down_weight, down_mean, down_square, grads[3], RATE_DOWN, DECAY_RATE),
        *adam_step(vectors, vector_mean, vector_square, vector_grad, RATE_VECTOR, 0.0),
        vector_grad,
    )


def solution(mesh):
    tokens = P(("dp", "row"), "col")
    qkv, proj, up, down, vec = P(None, "row", "col"), P("col", "row"), P("row", "col"), P("col", "row"), P(None, "col")
    return jax.shard_map(
        functools.partial(body, mesh.shape["dp"]),
        mesh=mesh,
        in_specs=(tokens, tokens, qkv, proj, up, down, vec, qkv, qkv, proj, proj, up, up, down, down, vec, vec),
        out_specs=(tokens, tokens) + (qkv,) * 3 + (proj,) * 3 + (up,) * 3 + (down,) * 3 + (vec,) * 4,
        check_vma=False,
    )
```

```python
import functools

import jax
import jax.numpy as jnp
from jax import lax
from jax.experimental import pallas as pl
from jax.experimental.pallas import tpu as pltpu
from jax.sharding import PartitionSpec as P

MESH = pl.DeviceIdType.MESH
BF = jnp.bfloat16
F32 = jnp.float32

D = 512
HEADS = 8
HEAD_DIM = 64
FF = 2048
SEQ = 512
STEP = 10
ROWS = 4
HALF = D // 2
BLK = D // ROWS
HID = 512

NORM_EPS = 1e-05
BETA_ONE = 0.9
BETA_TWO = 0.999
ADAM_EPS = 1e-08
DECAY_RATE = 0.01
RATE_QKV = 0.03
RATE_PROJ = 0.3
RATE_UP = 0.03
RATE_DOWN = 0.02
RATE_VECTOR = 0.3
VMEM_BYTES = 60 * 2**20

GATHER_UNITS = ((0, 0), (0, 1), (0, 2), (1, 0), (2, 0), (3, 0), (2, 1), (3, 1))
LEAD = {4: 0, 5: 1, 6: 1, 7: 0}
REDUCE_UNITS = ((3, 0), (2, 0), (3, 1), (2, 1), (1, 0), (0, 0), (0, 1), (0, 2))


def at(start, size, multiple=128):
    return pl.ds(pl.multiple_of(start, multiple), size)


def mm(a, b):
    return jnp.dot(a, b, preferred_element_type=F32)


def mm_lt(a, b):
    return lax.dot_general(a, b, (((0,), (0,)), ((), ())), preferred_element_type=F32)


def mm_rt(a, b):
    return lax.dot_general(a, b, (((1,), (1,)), ((), ())), preferred_element_type=F32)


def piece(unit, full, r, c):
    kind, k = unit
    if kind == 0:
        return full[0].at[k, at(r * BLK, BLK), at(c * HALF, HALF)]
    if kind == 1:
        return full[1].at[at(c * HALF, HALF), at(r * BLK, BLK)]
    if kind == 2:
        return full[2].at[at(r * BLK, BLK), at(c * 2 * HID + k * HID, HID)]
    return full[3].at[at(c * 2 * HID + k * HID, HID), at(r * BLK, BLK)]


def own_piece(unit, own):
    kind, k = unit
    if kind == 0:
        return own[0].at[k]
    if kind == 1:
        return own[1]
    if kind == 2:
        return own[2].at[:, pl.ds(k * HID, HID)]
    return own[3].at[pl.ds(k * HID, HID), :]


def column(unit, full, c):
    kind, k = unit
    if kind == 0:
        return full[0].at[k, :, at(c * HALF, HALF)]
    if kind == 1:
        return full[1].at[at(c * HALF, HALF), :]
    if kind == 2:
        return full[2].at[:, at(c * 2 * HID + k * HID, HID)]
    return full[3].at[at(c * 2 * HID + k * HID, HID), :]


def column_shape(unit):
    return ((D, HALF), (HALF, D), (D, HID), (HID, D))[unit[0]]


def piece_shape(unit):
    return ((BLK, HALF), (HALF, BLK), (BLK, HID), (HID, BLK))[unit[0]]


def row_part(unit, col_ref, r):
    if unit[0] in (0, 2):
        return col_ref.at[at(r * BLK, BLK), :]
    return col_ref.at[:, at(r * BLK, BLK)]


def remote(src, dst, send, recv, **where):
    return pltpu.make_async_remote_copy(
        src_ref=src, dst_ref=dst, send_sem=send, recv_sem=recv, device_id=where, device_id_type=MESH
    )


def position():
    return lax.axis_index("row"), lax.axis_index("col")


def flip(r, bit):
    if bit == 1:
        return r + 1 - 2 * lax.rem(r, 2)
    if bit == 2:
        return lax.rem(r + 2, 4)
    return 3 - r


def greet(dp_count):
    r, c = position()
    barrier = pltpu.get_barrier_semaphore()
    peers = [{"col": 1 - c}, {"row": flip(r, 1)}, {"row": flip(r, 2)}]
    if dp_count:
        z = lax.axis_index("dp")
        peers += [{"dp": lax.rem(z + k, dp_count)} for k in range(1, dp_count)]
    for peer in peers:
        pl.semaphore_signal(barrier, inc=1, device_id=peer, device_id_type=MESH)
    pl.semaphore_wait(barrier, len(peers))


def norm_forward(total):
    mean = jnp.mean(total, -1, keepdims=True)
    centered = total - mean
    scale = lax.rsqrt(jnp.mean(centered * centered, -1, keepdims=True) + NORM_EPS)
    return centered * scale, scale


def norm_back(grad, normed, scale, gain):
    scaled = grad * gain
    return scale * (
        scaled - jnp.mean(scaled, -1, keepdims=True) - normed * jnp.mean(scaled * normed, -1, keepdims=True)
    )


def col_sum(value):
    return jnp.sum(value, 0, keepdims=True)


def kernel(dp_count, *refs):
    n = len(REDUCE_UNITS)
    refs = list(refs)

    def take(count):
        out = refs[:count]
        del refs[:count]
        return out

    tok, cot, qkv_in, proj_in, up_in, down_in, vec_in = take(7)
    bo_out, ig_out, gqkv, gproj, gup, gdown, gvec = take(7)
    x_ref, ct_ref, qkv, proj, up, down, vec = take(7)
    own = take(4)
    bo, ig, dqkv, dproj, dup, ddown, vg = take(7)
    q_s, k_s, v_s, p_s, a_s, u_s, gp_s, h1_s, n1_s, da_s, dq_s, dk_s, dv_s = take(13)
    sib_buf, sums, buf_a, buf_b, send_b, zsrc, zbuf = (take(n) for _ in range(7))
    vsum, vbuf, send_in, recv_in, send_g, recv_g, send, recv, send_v, recv_v = take(10)
    full = (qkv, proj, up, down)
    grads, outs = (dqkv, dproj, dup, ddown), (gqkv, gproj, gup, gdown)
    r, c = position()
    sib = 1 - c
    z = lax.axis_index("dp") if dp_count else None
    started, started_end, started_mid = [], [], []
    if dp_count:
        middle = jnp.logical_or(z == 1, z == 2)
        end = jnp.logical_not(middle)

    def go(copy, kept=started):
        copy.start()
        kept.append(copy)
        return copy

    for src, dst in zip((qkv_in, proj_in, up_in, down_in), own):
        dst[...] = src[...].astype(BF)
    greet(dp_count)
    hops = {}
    started_lead = ([], [])
    if dp_count:
        parity = lax.rem(z, 2)

    def shared(u):
        return bool(dp_count) and u in LEAD

    def hop(u, slot, who, **where):
        unit = GATHER_UNITS[u]
        block = piece(unit, full, who, c)
        src = own_piece(unit, own) if slot in (0, 1, 3) else block
        return remote(src, block, send_g.at[u, slot], recv_g.at[u, slot], **where)

    def issue(u):
        x, y, far_row = flip(r, 1), flip(r, 2), flip(r, 3)
        hops[u] = {
            0: hop(u, 0, r, row=x),
            1: hop(u, 1, r, row=y),
            2: hop(u, 2, x if u % 2 == 0 else y, row=y if u % 2 == 0 else x),
            3: hop(u, 3, r, col=sib),
            4: hop(u, 4, x, col=sib),
            5: hop(u, 5, y, col=sib),
            6: hop(u, 6, far_row, col=sib),
        }
        go(hops[u][3])
        if not shared(u):
            go(hops[u][0])
            go(hops[u][1])
            return
        for k, who in enumerate((x, y, far_row)):
            hops[u][7 + k] = hop(u, 7 + k, who, dp=flip(z, 1))

        @pl.when(parity == LEAD[u])
        def _():
            go(hops[u][0], started_lead[LEAD[u]])
            go(hops[u][1], started_lead[LEAD[u]])

    def lead(u, act):
        if not shared(u):
            act(started)
        else:
            @pl.when(parity == LEAD[u])
            def _():
                act(started_lead[LEAD[u]])

    def near(u):
        def act(kept):
            for k in (0, 1):
                hops[u][k].wait_recv()
                if k == u % 2:
                    go(hops[u][2], kept)
                if shared(u):
                    go(hops[u][7 + k], kept)
                go(hops[u][4 + k], kept)

        lead(u, act)

    def far(u):
        def act(kept):
            hops[u][2].wait_recv()
            if shared(u):
                go(hops[u][9], kept)
            go(hops[u][6], kept)

        lead(u, act)

    def follow(u):
        if shared(u):
            @pl.when(parity != LEAD[u])
            def _():
                for k in range(3):
                    hops[u][7 + k].wait_recv()
                    go(hops[u][4 + k], started_lead[1 - LEAD[u]])

    def whole(u):
        for slot in (3, 4, 5, 6):
            hops[u][slot].wait_recv()

    ins = [
        go(remote(src.at[at(sib * SEQ, SEQ), :], dst.at[:, at(c * HALF, HALF)], send_in.at[i], recv_in.at[i], col=sib))
        for i, (src, dst) in enumerate(((tok, x_ref), (cot, ct_ref)))
    ]
    ins.append(go(remote(vec_in, vec.at[c], send_in.at[2], recv_in.at[2], col=sib)))
    for u in range(6):
        issue(u)
    for src, dst in ((tok, x_ref), (cot, ct_ref)):
        dst[:, at(c * HALF, HALF)] = src[at(c * SEQ, SEQ), :]
    vec[c] = vec_in[...]
    for unit in GATHER_UNITS:
        piece(unit, full, r, c)[...] = own_piece(unit, own)[...]

    flying = {}

    def wait(key):
        for copy in flying.pop(key):
            copy.wait_recv()

    def add(*views):
        total = views[0][...].astype(F32)
        for view in views[1:]:
            total = total + view[...].astype(F32)
        return total

    def phase(u, step):
        unit = REDUCE_UNITS[u]
        a, b = (1, 2) if u % 2 == 0 else (2, 1)
        out = own_piece(unit, outs)
        if step == 0:
            flying[u] = [go(remote(column(unit, grads, sib), sib_buf[u], send.at[u, 0], recv.at[u, 0], col=sib))]
        elif step == 1:
            wait(u)
            sums[u][...] = add(column(unit, grads, c), sib_buf[u]).astype(BF)
            peer = flip(r, a)
            flying[u] = [
                go(remote(row_part(unit, sums[u], who), buf_a[u].at[i], send.at[u, 1 + i], recv.at[u, 1 + i], row=peer))
                for i, who in ((1, flip(r, 3)), (0, peer))
            ]
        elif step == 2:
            wait(u)
            send_b[u][...] = add(row_part(unit, sums[u], flip(r, b)), buf_a[u].at[1]).astype(BF)
            flying[u] = [go(remote(send_b[u], buf_b[u], send.at[u, 3], recv.at[u, 3], row=flip(r, b)))]
        elif step == 3:
            wait(u)
            total = add(row_part(unit, sums[u], r), buf_a[u].at[0], buf_b[u]).astype(BF)
            if not dp_count:
                out[...] = total
                return
            zsrc[u][...] = total
            side = remote(zsrc[u], zbuf[u].at[0], send.at[u, 4], recv.at[u, 4], dp=flip(z, 1))
            inner = remote(zsrc[u], zbuf[u].at[1], send.at[u, 5], recv.at[u, 5], dp=3 - z)
            back = remote(out, out, send.at[u, 6], recv.at[u, 6], dp=flip(z, 1))
            flying[u] = (side, inner, back)

            @pl.when(end)
            def _():
                go(side, started_end)
        elif dp_count and step == 4:
            side, inner, back = flying[u]

            @pl.when(middle)
            def _():
                side.wait_recv()
                zsrc[u][...] = add(zsrc[u], zbuf[u].at[0]).astype(BF)
                go(inner, started_mid)
        elif dp_count and step == 5:
            side, inner, back = flying[u]

            @pl.when(middle)
            def _():
                inner.wait_recv()
                out[...] = add(zsrc[u], zbuf[u].at[1]).astype(BF)
                go(back, started_mid)
        elif dp_count:
            side, inner, back = flying[u]

            @pl.when(end)
            def _():
                back.wait_recv()

    def vec_step(step):
        if step == 0:
            flying["v"] = [go(remote(vg.at[sib], vbuf.at[0], send_v.at[2], recv_v.at[2], col=sib))]
        elif step == 1:
            wait("v")
            vsum[0] = vg[c] + vbuf[0]
            flying["v"] = [go(remote(vsum.at[0], vbuf.at[1], send_v.at[3], recv_v.at[3], row=flip(r, 1)))]
        elif step == 2:
            wait("v")
            vsum[1] = vsum[0] + vbuf[1]
            flying["v"] = [go(remote(vsum.at[1], vbuf.at[2], send_v.at[4], recv_v.at[4], row=flip(r, 2)))]
        elif step == 3:
            wait("v")
            total = vsum[1] + vbuf[2]
            if not dp_count:
                gvec[...] = total
                return
            vsum[2] = total
            flying["v"] = [
                go(remote(vsum.at[2], vbuf.at[2 + k], send_v.at[4 + k], recv_v.at[4 + k],
                          dp=lax.rem(z + k, dp_count)))
                for k in range(1, dp_count)
            ]
        elif step == 4 and dp_count:
            wait("v")
            parts = [vsum[2]] + [vbuf[2 + k] for k in range(1, dp_count)]
            total = jnp.zeros_like(parts[0])
            for owner in range(dp_count):
                for k, part in enumerate(parts):
                    total = total + jnp.where(lax.rem(z + dp_count - k, dp_count) == owner, part, 0.0)
            gvec[...] = total

    def stage(group, step):
        phase(2 * group, step)
        phase(2 * group + 1, step)

    def give_back(i, src, dst):
        copy = go(remote(src.at[:, at(sib * HALF, HALF)], dst.at[at(c * SEQ, SEQ), :],
                         send_v.at[i], recv_v.at[i], col=sib))
        dst[at(c * SEQ, SEQ), :] = src[:, at(c * HALF, HALF)]
        return copy

    def row(i):
        return jnp.concatenate([vec[0, i:i + 1, :], vec[1, i:i + 1, :]], 1)

    def put_row(i, value):
        vg[0, i:i + 1, :] = value[:, :HALF]
        vg[1, i:i + 1, :] = value[:, HALF:]

    near(0)
    issue(6)
    near(1)
    far(0)
    issue(7)
    near(2)
    far(1)
    for copy in ins:
        copy.wait_recv()
    whole(0)
    scaling = HEAD_DIM ** (-0.5)
    q_s[...] = (mm(x_ref[...], qkv[0]) + row(0)).astype(BF)
    far(2)
    whole(1)
    k_s[...] = mm(x_ref[...], qkv[1]).astype(BF)
    near(3)
    whole(2)
    v_s[...] = (mm(x_ref[...], qkv[2]) + row(1)).astype(BF)
    beside = {0: ((far, 3),), 1: ((near, 4), (near, 5)), 3: ((far, 4), (far, 5)), 5: ((follow, 4), (follow, 5)),
              7: ((near, 6), (near, 7))}
    for h in range(HEADS):
        cols = slice(h * HEAD_DIM, (h + 1) * HEAD_DIM)
        s = mm_rt(q_s[:, cols], k_s[:, cols]) * scaling
        e = jnp.exp(s - jnp.max(s, -1, keepdims=True))
        p = e * (1.0 / jnp.sum(e, -1, keepdims=True))
        p_s[h] = p
        a_s[:, cols] = mm(p.astype(BF), v_s[:, cols]).astype(BF)
        for act, u in beside.get(h, ()):
            act(u)
    whole(3)
    n1, scale1 = norm_forward(x_ref[...].astype(F32) + mm(a_s[...], proj[...]) + row(2))
    n1_s[...] = n1
    h1 = n1 * row(4) + row(5)
    h1_s[...] = h1.astype(BF)
    far(6)
    far(7)
    acc = h1 + row(3)
    for j in (0, 2, 1, 3):
        if j == 1:
            follow(6)
            follow(7)
        if j < 2:
            whole(4 + 2 * j)
            whole(5 + 2 * j)
        c_of, k = j // 2, 2 * (j % 2)
        bias = jnp.concatenate([vec[c_of, 8 + k:9 + k, :], vec[c_of, 9 + k:10 + k, :]], 1)
        cols = slice(j * HID, (j + 1) * HID)
        pre = mm(h1_s[...], up[:, cols]) + bias
        half = 0.5 + 0.5 * lax.erf(pre * 0.7071067811865476)
        u = (pre * half).astype(BF)
        u_s[:, cols] = u
        gp_s[:, cols] = half + pre * (0.3989422804014327 * jnp.exp(-0.5 * pre * pre))
        acc = acc + mm(u, down[cols, :])
    n2, scale2 = norm_forward(acc)
    bo[...] = (n2 * row(6) + row(7)).astype(BF)
    give = [give_back(0, bo, bo_out)]

    dy = ct_ref[...].astype(F32)
    put_row(6, col_sum(dy * n2))
    put_row(7, col_sum(dy))
    dr2 = norm_back(dy, n2, scale2, row(6))
    put_row(3, col_sum(dr2))
    g2 = dr2.astype(BF)
    ig[...] = dr2
    for j in (0, 2, 1, 3):
        c_of, k = j // 2, 2 * (j % 2)
        cols = slice(j * HID, (j + 1) * HID)
        ddown[cols, :] = mm_lt(u_s[:, cols], g2).astype(BF)
        if j >= 2:
            phase(2 * (j - 2), 0)
        dz = (mm_rt(g2, down[cols, :]) * gp_s[:, cols]).astype(BF)
        db = col_sum(dz.astype(F32))
        vg[c_of, 8 + k:9 + k, :] = db[:, :HALF]
        vg[c_of, 9 + k:10 + k, :] = db[:, HALF:]
        dup[:, cols] = mm_lt(h1_s[...], dz).astype(BF)
        if j >= 2:
            phase(2 * (j - 2) + 1, 0)
        if j == 1:
            stage(0, 1)
        ig[...] = ig[...] + mm_rt(dz, up[:, cols])
    acc = ig[...]
    n1 = n1_s[...]
    put_row(4, col_sum(acc * n1))
    put_row(5, col_sum(acc))
    dr1 = norm_back(acc, n1, scale1, row(4))
    put_row(2, col_sum(dr1))
    ig[...] = dr1
    g1 = dr1.astype(BF)
    dproj[...] = mm_lt(a_s[...], g1).astype(BF)
    phase(4, 0)
    da_s[...] = mm_rt(g1, proj[...]).astype(BF)
    for h in range(HEADS):
        cols = slice(h * HEAD_DIM, (h + 1) * HEAD_DIM)
        da = da_s[:, cols]
        p = p_s[h]
        dp = mm_rt(da, v_s[:, cols])
        ds = (p * (dp - jnp.sum(p * dp, -1, keepdims=True))).astype(BF)
        dq_s[:, cols] = (mm(ds, k_s[:, cols]) * scaling).astype(BF)
        dk_s[:, cols] = (mm_lt(ds, q_s[:, cols]) * scaling).astype(BF)
        dv_s[:, cols] = mm_lt(p.astype(BF), da).astype(BF)
        if h == 0:
            stage(0, 2)
            stage(1, 1)
        if h == 3:
            stage(0, 3)
        if h == 7:
            stage(1, 2)
            stage(0, 4)
    for i, (src, weight) in enumerate(((dq_s, 0), (dk_s, 1), (dv_s, 2))):
        grad = src[...]
        dqkv[weight] = mm_lt(x_ref[...], grad).astype(BF)
        phase(5 + i, 0)
        if i != 1:
            put_row(i // 2, col_sum(grad.astype(F32)))
    vec_step(0)
    stage(2, 1)
    stage(1, 3)
    stage(0, 5)
    ig[...] = ig[...] + mm_rt(dq_s[...], qkv[0]) + mm_rt(dk_s[...], qkv[1]) + mm_rt(dv_s[...], qkv[2])
    give.append(give_back(1, ig, ig_out))
    tail = (
        ((2, 2), (3, 1), (1, 4), (0, 6)),
        ((2, 3), (3, 2), (1, 5)),
        ((2, 4), (3, 3), (1, 6)),
        ((2, 5), (3, 4)),
        ((2, 6), (3, 5)),
        ((3, 6),),
    )
    for t, group in enumerate(tail):
        for pair in group:
            stage(*pair)
        if t < 4:
            vec_step(t + 1)
    for copy in give:
        copy.wait_recv()
    for copy in started:
        copy.wait_send()
    if dp_count:
        for side in (0, 1):
            @pl.when(parity == side)
            def _():
                for copy in started_lead[side]:
                    copy.wait_send()

        @pl.when(end)
        def _():
            for copy in started_end:
                copy.wait_send()

        @pl.when(middle)
        def _():
            for copy in started_mid:
                copy.wait_send()


def adam_step(weight, mean_old, square_old, gradient, step_rate, decay_rate):
    mean_new = BETA_ONE * mean_old + (1.0 - BETA_ONE) * gradient
    square_new = BETA_TWO * square_old + (1.0 - BETA_TWO) * gradient * gradient
    mean_hat = mean_new / (1.0 - BETA_ONE**STEP)
    square_hat = square_new / (1.0 - BETA_TWO**STEP)
    weight_new = weight - step_rate * (
        mean_hat / (jnp.sqrt(square_hat) + ADAM_EPS) + decay_rate * weight
    )
    return (weight_new, mean_new, square_new)


def shape(dims, dtype):
    return jax.ShapeDtypeStruct(dims, dtype)


def call(kernel, ins, outs, scratch, collective_id=None):
    vmem = pl.BlockSpec(memory_space=pltpu.VMEM)
    extra = {} if collective_id is None else dict(collective_id=collective_id, has_side_effects=True)
    return pl.pallas_call(
        kernel,
        out_shape=outs,
        in_specs=[vmem] * len(ins),
        out_specs=[vmem] * len(outs),
        scratch_shapes=scratch,
        compiler_params=pltpu.CompilerParams(vmem_limit_bytes=VMEM_BYTES, **extra),
    )(*ins)


FULL = ((3, D, D), (D, D), (D, FF), (FF, D))
OWN = ((3, BLK, HALF), (HALF, BLK), (BLK, FF // 2), (FF // 2, BLK))


def body(
    dp_size,
    tokens, cotangent, qkv_weight, proj_weight, up_weight, down_weight, vectors,
    qkv_mean, qkv_square, proj_mean, proj_square, up_mean, up_square,
    down_mean, down_square, vector_mean, vector_square,
):
    dma, vm = pltpu.SemaphoreType.DMA, pltpu.VMEM
    n = len(REDUCE_UNITS)
    dp_count = dp_size if dp_size == 4 else 0
    pieces = [piece_shape(u) for u in REDUCE_UNITS]
    columns = [column_shape(u) for u in REDUCE_UNITS]
    sq, whole = vm((SEQ, D), BF), [vm(s, BF) for s in FULL]
    reduced = call(
        functools.partial(kernel, dp_count),
        (tokens, cotangent, qkv_weight, proj_weight, up_weight, down_weight, vectors),
        [shape((2 * SEQ, HALF), BF), shape((2 * SEQ, HALF), F32)] + [shape(s, BF) for s in OWN]
        + [shape((12, HALF), F32)],
        [sq, sq] + whole + [vm((2, 12, HALF), F32)]
        + [vm(s, BF) for s in OWN]
        + [sq, vm((SEQ, D), F32)] + whole + [vm((2, 12, HALF), F32)]
        + [sq, sq, sq, vm((HEADS, SEQ, SEQ), F32), sq, vm((SEQ, FF), BF), vm((SEQ, FF), F32), sq,
           vm((SEQ, D), F32), sq, sq, sq, sq]
        + [vm(s, BF) for s in columns] * 2
        + [vm((2,) + s, BF) for s in pieces] + [vm(s, BF) for s in pieces] * 3 + [vm((2,) + s, BF) for s in pieces]
        + [vm((3, 12, HALF), F32), vm((6, 12, HALF), F32),
           dma((3,)), dma((3,)), dma((n, 10)), dma((n, 10)), dma((n, 7)), dma((n, 7)), dma((8,)), dma((8,))],
        collective_id=0,
    )
    output, input_grad, grads, vector_grad = reduced[0], reduced[1], reduced[2:6], reduced[6]
    grads = [g.astype(F32) for g in grads]
    if not dp_count:
        grads = [lax.psum(g, "dp") for g in grads]
        vector_grad = lax.psum(vector_grad, "dp")
    return (
        output,
        input_grad,
        *adam_step(qkv_weight, qkv_mean, qkv_square, grads[0], RATE_QKV, DECAY_RATE),
        *adam_step(proj_weight, proj_mean, proj_square, grads[1], RATE_PROJ, DECAY_RATE),
        *adam_step(up_weight, up_mean, up_square, grads[2], RATE_UP, DECAY_RATE),
        *adam_step(down_weight, down_mean, down_square, grads[3], RATE_DOWN, DECAY_RATE),
        *adam_step(vectors, vector_mean, vector_square, vector_grad, RATE_VECTOR, 0.0),
        vector_grad,
    )


def solution(mesh):
    tokens = P(("dp", "row"), "col")
    qkv, proj, up, down, vec = P(None, "row", "col"), P("col", "row"), P("row", "col"), P("col", "row"), P(None, "col")
    return jax.shard_map(
        functools.partial(body, mesh.shape["dp"]),
        mesh=mesh,
        in_specs=(tokens, tokens, qkv, proj, up, down, vec, qkv, qkv, proj, proj, up, up, down, down, vec, vec),
        out_specs=(tokens, tokens) + (qkv,) * 3 + (proj,) * 3 + (up,) * 3 + (down,) * 3 + (vec,) * 4,
        check_vma=False,
    )
```
